32 devices in a mesh: row: 4 (over y, x), col: 8 (over z, core).
Axes of the slice: x: 2, y: 2, z: 4, core: 2. Of those that a mesh axis runs over, the one named last changes fastest.
Arguments:
- eigenvectors: float32 [1536, 61440], P('col', 'row'), may hold values from -6 to 6
- householder: float32 [2, 128, 61440], P(None, 'col', 'row'), may hold values from -0.5 to 0.5
- factors: float32 [2, 128, 128], replicated, may hold values from -0.0234375 to 0.0234375
Outputs:
- transformed: float32 [1536, 61440], P('col', 'row')
The draws below stay inside these ranges and needn't reach their ends.
All inputs are finite; a program needn't handle non-finite values.
Results may differ from the reference program's by a relative error of at most 0.0001.
Values sent between devices are 32-bit elements; how exact they have to be, the bound alone decides.
No kernel may reach another device: no remote copies, remote signals or barrier semaphores. Data moves between devices by JAX's collectives and lax.ppermute only.
A program may use at most 128 MiB of HBM per device.

```python
import jax
import jax.numpy as jnp
from jax import lax

NEV = 1536
NB = 128
NBLK = 2
NROWS = 61440


def shard_levels(key, shape, split, least, high):
    def one(dim, blocks):
        steps = jax.random.uniform(jax.random.fold_in(jax.random.fold_in(key, 6), dim), (blocks,), jnp.float32, least / len(split), high / len(split))
        return jnp.repeat(jnp.exp(steps), shape[dim] // blocks).reshape((-1,) + (1,) * (len(shape) - dim - 1))

    gain = one(*split[0])
    for cut in split[1:]:
        gain = gain * one(*cut)
    return gain


def bell_draw(key, extent, width, bound, pieces=(), dtype=jnp.bfloat16):
    gain = shard_levels(key, extent, pieces, -0.22, 0.18) if pieces else 1.0
    entries = jax.random.normal(key, extent, jnp.float32) * width * gain
    return jnp.minimum(jnp.maximum(entries, -bound), bound).astype(dtype)


def setup_inputs(seed: int = 0) -> dict:
    key_list = jax.random.split(jax.random.key(seed), 4)
    return {
        "eigenvectors": bell_draw(key_list[0], (NEV, NROWS), 1.0, 6.0, ((0, 8), (1, 4)), jnp.float32),
        "householder": bell_draw(key_list[1], (NBLK, NB, NROWS), NB ** -0.5, 0.5, ((1, 8), (2, 4)), jnp.float32),
        "factors": bell_draw(key_list[2], (NBLK, NB, NB), NROWS ** -0.5, 0.0234375, (), jnp.float32),
    }


def reference(eigenvectors, householder, factors):
    slab = eigenvectors
    for block in range(NBLK):
        upper = jnp.triu(factors[block])
        vectors = householder[block]
        projection = jnp.dot(vectors, slab.T, precision=lax.Precision.HIGHEST, preferred_element_type=jnp.float32)
        coeffs = jnp.dot(upper, projection, precision=lax.Precision.HIGHEST, preferred_element_type=jnp.float32)
        slab = slab - jnp.dot(coeffs.T, vectors, precision=lax.Precision.HIGHEST, preferred_element_type=jnp.float32)
    return slab
```

```python
import functools

import jax
import jax.numpy as jnp
from jax import lax
from jax.experimental import pallas as pl
from jax.experimental.pallas import tpu as pltpu
from jax.sharding import PartitionSpec as P

F32 = jnp.float32
BF16 = jnp.bfloat16
NT = (((1,), (1,)), ((), ()))
NN = (((1,), (0,)), ((), ()))
TILE = 1280
PARTS = 4
VMEM = 48 * 1024 * 1024


def split(x):
    high = x.astype(BF16)
    return high, (x - high.astype(F32)).astype(BF16)


def dot3(left, right, dims):
    (lh, ll), (rh, rl) = left, right
    dot = functools.partial(lax.dot_general, dimension_numbers=dims, preferred_element_type=F32)
    return dot(lh, rh) + (dot(ll, rh) + dot(lh, rl))


def exact(left, right, dims=NN):
    return lax.dot_general(left, right, dims, precision=lax.Precision.HIGHEST, preferred_element_type=F32)


def rows_of(refs, pick):
    return jnp.concatenate([refs[i][...] if b is None else refs[i][b] for i, b in pick], axis=0)


def project_kernel(pick, slab_ref, *refs):
    *pieces, out_ref = refs

    @pl.when(pl.program_id(0) == 0)
    def _():
        out_ref[...] = jnp.zeros_like(out_ref)

    out_ref[...] += dot3(split(rows_of(pieces, pick)), split(slab_ref[...]), NT)


def piece_spec(piece, tile, index):
    if piece.ndim == 2:
        return pl.BlockSpec((piece.shape[0], tile), lambda g: (0, index(g)))
    return pl.BlockSpec((2, piece.shape[1], tile), lambda g: (0, 0, index(g)))


def project(slab, pieces, pick, first=0):
    width = pieces[0].shape[-1]
    height = 16 * len(pick)
    count = width // TILE
    return pl.pallas_call(
        functools.partial(project_kernel, pick),
        out_shape=jax.ShapeDtypeStruct((height, slab.shape[0]), F32),
        grid=(count,),
        in_specs=[pl.BlockSpec((slab.shape[0], TILE), lambda g: (0, first + g))]
        + [piece_spec(p, TILE, lambda g: g) for p in pieces],
        out_specs=pl.BlockSpec((height, slab.shape[0]), lambda g: (0, 0)),
        compiler_params=pltpu.CompilerParams(vmem_limit_bytes=VMEM),
        cost_estimate=pl.CostEstimate(
            flops=6 * height * slab.shape[0] * width, bytes_accessed=4 * (height + slab.shape[0]) * width, transcendentals=0
        ),
        name="project",
    )(slab, *pieces)


def cross_kernel(low, high, *refs):
    *pieces, out_ref = refs

    @pl.when(pl.program_id(0) == 0)
    def _():
        out_ref[...] = jnp.zeros_like(out_ref)

    out_ref[...] += dot3(split(rows_of(pieces, high)), split(rows_of(pieces, low)), NT)


def cross(pieces, low, high):
    width = pieces[0].shape[-1]
    n = 16 * len(low)
    return pl.pallas_call(
        functools.partial(cross_kernel, low, high),
        out_shape=jax.ShapeDtypeStruct((n, n), F32),
        grid=(width // TILE,),
        in_specs=[piece_spec(p, TILE, lambda g: g) for p in pieces],
        out_specs=pl.BlockSpec((n, n), lambda g: (0, 0)),
        compiler_params=pltpu.CompilerParams(vmem_limit_bytes=VMEM),
        cost_estimate=pl.CostEstimate(flops=6 * n * n * width, bytes_accessed=8 * n * width, transcendentals=0),
        name="cross",
    )(*pieces)


def update_kernel(early, pick, per, slab_ref, upper_ref, cross_ref, known_ref, a_ref, b_ref, c_ref, d_ref, *refs):
    *pieces, out_ref, high_ref, low_ref = refs
    step = pl.program_id(0)

    @pl.when(step == 0)
    def _():
        last = (a_ref[...] + b_ref[...]) + (c_ref[...] + d_ref[...])
        half = last.shape[0] // 2
        one = jnp.concatenate([known_ref[0], last[:half]], axis=0)
        two = jnp.concatenate([known_ref[1], last[half:]], axis=0)
        first = exact(upper_ref[0], one)
        second = exact(upper_ref[1], two - exact(cross_ref[...], first))
        high, low = split(jnp.concatenate([first, second], axis=0).T)
        high_ref[...] = high
        low_ref[...] = low

    for part in range(len(pick)):

        @pl.when(step // per == part)
        def _():
            vectors = split(rows_of(pieces, pick[part]))
            out_ref[...] = slab_ref[...] - dot3((high_ref[...], low_ref[...]), vectors, NN)


def update(slab, upper, gram, known, lasts, pieces, parts, pick, pick_part):
    nev, width = slab.shape
    per = parts[0][0].shape[-1] // TILE
    operands = list(pieces)
    specs = [piece_spec(p, TILE, lambda g: g) for p in pieces]
    for i, part in enumerate(parts):
        operands += part
        specs += [piece_spec(p, TILE, lambda g, i=i: jnp.clip(g - i * per, 0, per - 1)) for p in part]
    whole = lambda x: pl.BlockSpec(x.shape, lambda g: (0,) * x.ndim)
    small = [upper, gram, known, *lasts]
    picks = [
        tuple(
            pick[b] + tuple((len(pieces) + i * len(parts[0]) + at, bb) for at, bb in pick_part[b]) for b in (0, 1)
        )
        for i in range(len(parts))
    ]
    n = sum(16 * len(r) for r in picks[0])
    return pl.pallas_call(
        functools.partial(update_kernel, None, [a + b for a, b in picks], per),
        out_shape=jax.ShapeDtypeStruct(slab.shape, F32),
        grid=(width // TILE,),
        in_specs=[pl.BlockSpec((nev, TILE), lambda g: (0, g))] + [whole(x) for x in small] + specs,
        out_specs=pl.BlockSpec((nev, TILE), lambda g: (0, g)),
        scratch_shapes=[pltpu.VMEM((nev, n), BF16), pltpu.VMEM((nev, n), BF16)],
        compiler_params=pltpu.CompilerParams(vmem_limit_bytes=VMEM),
        cost_estimate=pl.CostEstimate(
            flops=6 * n * nev * width, bytes_accessed=4 * (2 * nev + n) * width, transcendentals=0
        ),
        name="update",
    )(slab, *small, *operands)


def others(x):
    return [lax.ppermute(x, "row", [(i, i ^ k) for i in range(4)]) for k in (1, 2, 3)]


def sum_row(x):
    a, b, c = others(x)
    return (x + a) + (b + c)


def cores(pairs):
    return [(2 * a + c, 2 * b + c) for a, b in pairs for c in (0, 1)]


PAIR = cores([(0, 1), (1, 0), (2, 3), (3, 2)])
MIDDLE = cores([(1, 2), (2, 1)])
OUTWARD = cores([(1, 0), (2, 3)])
SIBLING = [(i, i ^ 1) for i in range(8)]


def along(x, pairs):
    return lax.ppermute(x, "col", pairs)


def line_of_four(slab, householder, factors):
    col = lax.axis_index("col")
    count, mine, width = householder.shape
    own = [householder[0], householder[1]]
    beside = [along(x, PAIR) for x in own]
    inner = [along(x, MIDDLE) for x in own]
    outer = [along(x, OUTWARD) for x in inner]
    across = [along(x, MIDDLE) for x in beside]
    third = [a + b for a, b in zip(outer, across)]
    step = width // PARTS
    cut = lambda pair, q: jnp.stack([x[:, q * step : (q + 1) * step] for x in pair])
    parts = []
    for q in range(PARTS):
        part = along(cut(across, q), OUTWARD) + cut(inner, q)
        parts.append([part, along(part, SIBLING)])

    other = along(householder, SIBLING)
    beside2 = [along(x, SIBLING) for x in beside]
    third2 = [along(x, SIBLING) for x in third]
    inner2 = [along(x, SIBLING) for x in inner]

    nev = slab.shape[0]
    four = ((0, 0), (1, 0), (0, 1), (1, 1))
    split4 = ((0, None), (2, None), (1, None), (3, None))
    p0 = project(slab, [householder, other], four).reshape(2, 2 * mine, nev)
    p1 = project(slab, beside + beside2, split4).reshape(2, 2 * mine, nev)
    p2 = project(slab, third + third2, split4).reshape(2, 2 * mine, nev)
    known = sum_row(jnp.concatenate([p0, p1, p2], axis=1))
    last = sum(project(slab, part, four, q * (step // TILE)) for q, part in enumerate(parts))
    lasts = [last, *others(last)]

    pieces = [householder, other, *beside, *beside2, *third, *third2]
    pick = [((0, b), (1, b), (2 + b, None), (4 + b, None), (6 + b, None), (8 + b, None)) for b in (0, 1)]
    full = [pick[b] + ((10 + b, None), (12 + b, None)) for b in (0, 1)]
    gram = sum_row(cross(pieces + inner + inner2, full[0], full[1]))
    given = along(gram, OUTWARD).reshape(2, 2, 2, mine, 2, 2, 2, mine)
    given = given[:, ::-1, :, :, :, ::-1].reshape(gram.shape)
    middle = jnp.logical_and(col >= 2, col < 6)
    gram = jnp.where(middle, gram, given)

    order = jnp.bitwise_xor(col, jnp.arange(8))
    upper = jnp.triu(factors).reshape(2, 8, mine, 8, mine)
    upper = jnp.take(jnp.take(upper, order, axis=1), order, axis=3).reshape(factors.shape)

    pick_part = [((0, b), (1, b)) for b in (0, 1)]
    return update(slab, upper, gram, known, lasts, pieces, parts, pick, pick_part)


def matmul(left, right):
    return jnp.dot(left, right, precision=lax.Precision.HIGHEST, preferred_element_type=F32)


def any_mesh(slab, householder, factors):
    upper = jnp.triu(factors)
    for block in range(householder.shape[0]):
        vectors = lax.all_gather(householder[block], "col", axis=0, tiled=True)
        projection = lax.psum(exact(vectors, slab, NT), "row")
        coeffs = matmul(upper[block], projection)
        slab = slab - exact(coeffs, vectors, (((0,), (0,)), ((), ())))
    return slab


def solution(mesh):
    small = mesh.shape["col"] == 8 and mesh.shape["row"] == 4
    return jax.shard_map(
        line_of_four if small else any_mesh,
        mesh=mesh,
        in_specs=(P("col", "row"), P(None, "col", "row"), P()),
        out_specs=P("col", "row"),
        check_vma=False,
    )
```

```python
import functools

import jax
import jax.numpy as jnp
from jax import lax
from jax.experimental import pallas as pl
from jax.experimental.pallas import tpu as pltpu
from jax.sharding import PartitionSpec as P

F32 = jnp.float32
BF16 = jnp.bfloat16
NT = (((1,), (1,)), ((), ()))
NN = (((1,), (0,)), ((), ()))
MIB = 1024 * 1024
TILE = 2560
WIDTHS = (5, 1)
COST = dict(join=10**6, project=10**9, cross=10**9, prepare=10**6, update=10**9)


def split(x):
    high = x.astype(BF16)
    return high, (x - high.astype(F32)).astype(BF16)


def dot3(left, right, dims):
    (lh, ll), (rh, rl) = left, right
    dot = functools.partial(lax.dot_general, dimension_numbers=dims, preferred_element_type=F32)
    return dot(lh, rh) + (dot(ll, rh) + dot(lh, rl))


def exact(left, right, dims=NN):
    return lax.dot_general(left, right, dims, precision=lax.Precision.HIGHEST, preferred_element_type=F32)


def block_rows(refs):
    return jnp.concatenate([r[b] for b in (0, 1) for r in refs], axis=0)


def total(refs):
    a, b, c, d = (r[...] for r in refs)
    return (a + b) + (c + d)


def whole(x):
    return pl.BlockSpec(x.shape, lambda g: (0,) * x.ndim)


def columns(x, at=0):
    lead = x.shape[:-1]
    return pl.BlockSpec(lead + (TILE,), lambda g: (0,) * len(lead) + (at // TILE + g,))


def call(kernel, steps, operands, specs, outs, out_specs, name, scratch=(), vmem=16):
    return pl.pallas_call(
        kernel,
        out_shape=outs,
        grid=(steps,),
        in_specs=specs,
        out_specs=out_specs,
        scratch_shapes=list(scratch),
        compiler_params=pltpu.CompilerParams(vmem_limit_bytes=vmem * MIB),
        cost_estimate=pl.CostEstimate(flops=COST[name], bytes_accessed=1, transcendentals=0),
        name=name,
    )(*operands)


def corner(x):
    lead = x.ndim - 2
    return pl.BlockSpec((1,) * lead + (8, 128), lambda g: (0,) * x.ndim)


def join_kernel(a_ref, b_ref, *refs):
    refs[-1][...] = a_ref[...] + b_ref[...]


def join(a, b, at, *after):
    out = jax.ShapeDtypeStruct(a.shape, F32)
    return call(
        join_kernel,
        a.shape[-1] // TILE,
        [a, b, *after],
        [columns(a), columns(b, at)] + [corner(y) for y in after],
        out,
        columns(out),
        "join",
    )


def project_kernel(steps, started, slab_ref, *refs):
    before, refs = (refs[0], refs[1:]) if started else (None, refs)
    *pieces, proj_ref, acc_ref = refs
    step = pl.program_id(0)

    @pl.when(step == 0)
    def _():
        acc_ref[...] = jnp.zeros_like(acc_ref)

    high, low = split(block_rows(pieces))
    slab_high, slab_low = split(slab_ref[...])
    n = high.shape[0]
    dot = functools.partial(lax.dot_general, dimension_numbers=NT, preferred_element_type=F32)
    both = dot(slab_high, jnp.concatenate([high, low], axis=0))
    acc_ref[...] += both[:, :n] + (both[:, n:] + dot(slab_low, high))

    @pl.when(step == steps - 1)
    def _():
        made = acc_ref[...].T
        proj_ref[...] = made + before[...] if started else made


def project(slab, pieces, at=0, before=None):
    nev = slab.shape[0]
    mine, width = pieces[0].shape[1:]
    steps = width // TILE
    rows = 2 * mine * len(pieces)
    out = jax.ShapeDtypeStruct((rows, nev), F32)
    small = [] if before is None else [before]
    return call(
        functools.partial(project_kernel, steps, bool(small)),
        steps,
        [slab, *small, *pieces],
        [columns(slab, at)] + [whole(x) for x in small] + [columns(p) for p in pieces],
        out,
        whole(out),
        "project",
        [pltpu.VMEM((nev, rows), F32)],
    )


def cross_kernel(*refs):
    *pieces, gram_ref = refs

    @pl.when(pl.program_id(0) == 0)
    def _():
        gram_ref[...] = jnp.zeros_like(gram_ref)

    high, low = split(block_rows(pieces))
    half = high.shape[0] // 2
    gram_ref[...] += dot3((high[half:], low[half:]), (high[:half], low[:half]), NT)


def cross(pieces):
    mine, width = pieces[0].shape[1:]
    n = mine * len(pieces)
    out = jax.ShapeDtypeStruct((n, n), F32)
    return call(cross_kernel, width // TILE, pieces, [columns(p) for p in pieces], out, whole(out), "cross")


def swap_matrix(n, mask):
    row = lax.broadcasted_iota(jnp.int32, (n, n), 0)
    column = lax.broadcasted_iota(jnp.int32, (n, n), 1)
    return jnp.where(column == jnp.bitwise_xor(row, mask), 1.0, 0.0).astype(F32)


def prepare_kernel(mine, col_ref, factors_ref, gram_ref, given_ref, *refs):
    sums, (known_ref, mats_ref) = refs[:8], refs[8:]
    n = factors_ref.shape[1]
    swap = swap_matrix(n, col_ref[0] * mine)
    row = lax.broadcasted_iota(jnp.int32, (n, n), 0)
    column = lax.broadcasted_iota(jnp.int32, (n, n), 1)
    for block in range(2):
        upper = jnp.where(row <= column, factors_ref[block], 0.0)
        mats_ref[block] = exact(swap, exact(upper, swap))
    turn = swap_matrix(n, 2 * mine)
    middle = jnp.logical_and(col_ref[0] >= 2, col_ref[0] < 6)
    mats_ref[2] = jnp.where(middle, gram_ref[...], exact(turn, exact(given_ref[...], turn)))
    first, second = total(sums[:4]), total(sums[4:])
    known_ref[...] = jnp.concatenate([x[b * x.shape[0] // 2 :][: x.shape[0] // 2] for b in (0, 1) for x in (first, second)], axis=0)


def prepare(col, factors, gram, given, sums, mine):
    small = [factors, gram, given, *sums[0], *sums[1]]
    outs = [
        jax.ShapeDtypeStruct((sum(s[0].shape[0] for s in sums), sums[0][0].shape[1]), F32),
        jax.ShapeDtypeStruct((3, *gram.shape), F32),
    ]
    return call(
        functools.partial(prepare_kernel, mine),
        1,
        [col[None], *small],
        [pl.BlockSpec(memory_space=pltpu.SMEM)] + [whole(x) for x in small],
        outs,
        [whole(x) for x in outs],
        "prepare",
    )


def update_kernel(starts, base, known_ref, mats_ref, *refs):
    lasts, (slab_ref, *pieces, out_ref, left_ref) = refs[:4], refs[4:]
    step = pl.program_id(0)

    @pl.when(step == 0)
    def _():
        last = total(lasts)
        kept, rest = known_ref.shape[0] // 2, last.shape[0] // 2
        half = lambda b: jnp.concatenate([known_ref[b * kept : (b + 1) * kept], last[b * rest : (b + 1) * rest]], axis=0)
        first = exact(mats_ref[0], half(0))
        second = exact(mats_ref[1], half(1) - exact(mats_ref[2], first))
        high, low = split(jnp.concatenate([first, second], axis=0).T)
        left_ref[...] = jnp.concatenate([high, low, high], axis=1)

    each = (len(pieces) - base) // (len(starts) - 1)
    for i in range(len(starts) - 1):

        @pl.when(jnp.logical_and(step >= starts[i], step < starts[i + 1]))
        def _():
            high, low = split(block_rows(pieces[:base] + pieces[base + each * i : base + each * (i + 1)]))
            right = jnp.concatenate([high, high, low], axis=0)
            out_ref[...] = slab_ref[...] - lax.dot_general(left_ref[...], right, NN, preferred_element_type=F32)


def update(known, mats, lasts, slab, pieces, parts):
    mine = pieces[0].shape[1]
    nev, width = slab.shape
    small = [known, mats, *lasts]
    starts, specs = [0], []
    for part in parts:
        first, count = starts[-1], part[0].shape[-1] // TILE
        starts.append(first + count)
        specs += [
            pl.BlockSpec((2, mine, TILE), lambda g, first=first, count=count: (0, 0, jnp.clip(g - first, 0, count - 1)))
            for x in part
        ]
    stay = [pltpu.with_memory_space_constraint(x, pltpu.HBM) for x in (slab, *pieces)]
    return call(
        functools.partial(update_kernel, starts, len(pieces)),
        width // TILE,
        [*small, *stay, *[x for part in parts for x in part]],
        [whole(x) for x in small] + [columns(x) for x in (slab, *pieces)] + specs,
        jax.ShapeDtypeStruct(slab.shape, F32),
        columns(slab),
        "update",
        [pltpu.VMEM((nev, 6 * mats.shape[1]), BF16)],
        vmem=32,
    )


def others(x):
    return [lax.ppermute(x, "row", [(i, i ^ k) for i in range(4)]) for k in (1, 2, 3)]


def cores(pairs):
    return [(2 * a + c, 2 * b + c) for a, b in pairs for c in (0, 1)]


PAIR = cores([(0, 1), (1, 0), (2, 3), (3, 2)])
MIDDLE = cores([(1, 2), (2, 1)])
OUTWARD = cores([(1, 0), (2, 3)])
SIBLING = [(i, i ^ 1) for i in range(8)]


def along(x, pairs):
    return lax.ppermute(x, "col", pairs)


def line_of_four(slab, householder, factors):
    col = lax.axis_index("col")
    mine, width = householder.shape[1:]
    swap = lambda x: along(x, SIBLING)
    other = swap(householder)

    beside, inner = along(householder, PAIR), along(householder, MIDDLE)
    across, outer = along(beside, MIDDLE), along(inner, OUTWARD)
    stretches = [(sum(WIDTHS[:i]) * TILE, w * TILE) for i, w in enumerate(WIDTHS)]
    final = [along(across if w == width else across[:, :, at : at + w], OUTWARD) for at, w in stretches]
    inner2 = swap(inner)

    near = [householder, other, beside, swap(beside)]
    p0 = project(slab, near)
    sums0 = [p0, *others(p0)]
    third = join(outer, across, 0, *sums0)
    third = [third, swap(third)]
    p1 = project(slab, third)
    gram = cross(near + third + [inner, inner2])
    sums1 = [p1, *others(p1)]
    a, b, c = others(gram)
    gram = (gram + a) + (b + c)
    known, mats = prepare(col, factors, gram, along(gram, OUTWARD), [sums0, sums1], mine)

    last, parts, behind = None, [], [known]
    for i, (at, w) in enumerate(stretches):
        fourth = join(final[i], inner, at, *behind)
        parts.append([fourth, swap(fourth)])
        last = project(slab, parts[-1], at, last)
        behind = [last]
    return update(known, mats, [last, *others(last)], slab, near + third, parts)


def any_mesh(slab, householder, factors):
    upper = jnp.triu(factors)
    for block in range(householder.shape[0]):
        vectors = lax.all_gather(householder[block], "col", axis=0, tiled=True)
        projection = lax.psum(exact(vectors, slab, NT), "row")
        coeffs = exact(upper[block], projection)
        slab = slab - exact(coeffs, vectors, (((0,), (0,)), ((), ())))
    return slab


def solution(mesh):
    small = mesh.shape["col"] == 8 and mesh.shape["row"] == 4
    return jax.shard_map(
        line_of_four if small else any_mesh,
        mesh=mesh,
        in_specs=(P("col", "row"), P(None, "col", "row"), P()),
        out_specs=P("col", "row"),
        check_vma=False,
    )
```

```python
import functools

import jax
import jax.numpy as jnp
from jax import lax
from jax.experimental import pallas as pl
from jax.experimental.pallas import tpu as pltpu
from jax.sharding import PartitionSpec as P

F32 = jnp.float32
BF16 = jnp.bfloat16
NT = (((1,), (1,)), ((), ()))
NN = (((1,), (0,)), ((), ()))
MIB = 1024 * 1024
TILE = 2560
WIDTHS = (4, 2)
COST = dict(settle=10**6, hold=10**9, join=10**6, take=10**6, project=10**9, cross=10**9, weigh=10**6, apply=10**9, finish=10**9)
FINISH = 16
MADE = jax.ShapeDtypeStruct


def split(x):
    high = x.astype(BF16)
    return high, (x - high.astype(F32)).astype(BF16)


def wide3(left, right):
    (lh, ll), (rh, rl) = left, right
    dot = functools.partial(lax.dot_general, dimension_numbers=NT, preferred_element_type=F32)
    n = rh.shape[0]
    both = dot(lh, jnp.concatenate([rh, rl], axis=0))
    return both[:, :n] + (both[:, n:] + dot(ll, rh))


def exact(left, right, dims=NN):
    return lax.dot_general(left, right, dims, precision=lax.Precision.HIGHEST, preferred_element_type=F32)


def block_rows(refs):
    return jnp.concatenate([r[b] for b in (0, 1) for r in refs], axis=0)


def total(refs):
    a, b, c, d = (r[...] for r in refs)
    return (a + b) + (c + d)


def whole(x):
    return pl.BlockSpec(x.shape, lambda g: (0,) * x.ndim)


def columns(x, at=0):
    lead = x.shape[:-1]
    return pl.BlockSpec(lead + (TILE,), lambda g: (0,) * len(lead) + (at // TILE + g,))


HELD = pl.BlockSpec(memory_space=pltpu.VMEM)


def held(x):
    return pltpu.with_memory_space_constraint(x, pltpu.VMEM)


def tile_of(ref):
    return ref[:, pl.ds(pl.multiple_of(pl.program_id(0) * TILE, TILE), TILE)]


def call(kernel, steps, operands, specs, outs, out_specs, name, scratch=(), vmem=16):
    return pl.pallas_call(
        kernel,
        out_shape=outs,
        grid=(steps,),
        in_specs=specs,
        out_specs=out_specs,
        scratch_shapes=list(scratch),
        compiler_params=pltpu.CompilerParams(vmem_limit_bytes=vmem * MIB),
        cost_estimate=pl.CostEstimate(flops=COST[name], bytes_accessed=1, transcendentals=0),
        name=name,
    )(*operands)


def still(x):
    return pltpu.with_memory_space_constraint(x, pltpu.HBM)


def corner(x):
    lead = x.ndim - 2
    return pl.BlockSpec((1,) * lead + (8, 128), lambda g: (0,) * x.ndim)


def join_kernel(count, a_ref, b_ref, *refs):
    out_ref, cut_ref = refs[-2:]
    out_ref[...] = a_ref[...] + b_ref[...]

    @pl.when(pl.program_id(0) < count)
    def _():
        cut_ref[...] = out_ref[...]


def join(a, b, count, *after):
    out, cut = MADE(a.shape, F32), MADE((*a.shape[:-1], count * TILE), F32)
    return call(
        functools.partial(join_kernel, count),
        a.shape[-1] // TILE,
        [a, b, *after],
        [columns(a), columns(b)] + [corner(y) for y in after],
        [out, cut],
        [columns(out), pl.BlockSpec((*a.shape[:-1], TILE), lambda g: (0, 0, jnp.minimum(g, count - 1)))],
        "join",
    )


def hold_kernel(x_ref, out_ref):
    out_ref[...] = x_ref[...]


def hold(x):
    out = pltpu.VMEM(x.shape, F32)
    return call(hold_kernel, x.shape[-1] // TILE, [still(x)], [columns(x)], out, columns(x), "hold")


def settle_kernel(*refs):
    refs[-1][...] = total(refs[:-1])


def settle(*parts):
    return call(settle_kernel, 1, parts, [whole(x) for x in parts], MADE(parts[0].shape, F32), whole(parts[0]), "settle")


def settle_both_kernel(a_ref, b_ref, c_ref, d_ref, gram_ref, proj_ref):
    n, rows = gram_ref.shape[0], proj_ref.shape[0]
    both = total([a_ref, b_ref, c_ref, d_ref])
    gram_ref[...] = both[:, :n]
    proj_ref[...] = jnp.concatenate([both[:rows, n:], both[rows:, n:]], axis=1)


def settle_both(parts, rows, nev):
    n = parts[0].shape[0]
    outs = [MADE((n, n), F32), MADE((rows, nev), F32)]
    return call(settle_both_kernel, 1, parts, [whole(x) for x in parts], outs, [whole(x) for x in outs], "settle")


def take_kernel(x_ref, *refs):
    refs[-1][...] = x_ref[...]


def take(x, at, width, *after):
    out = jax.ShapeDtypeStruct((*x.shape[:-1], width), F32)
    return call(
        take_kernel, width // TILE, [x, *after], [columns(x, at)] + [corner(y) for y in after], out, columns(out), "take"
    )


def project_kernel(steps, lies, started, slab_ref, *refs):
    before, refs = (refs[0], refs[1:]) if started else (None, refs)
    *pieces, proj_ref, acc_ref = refs
    step = pl.program_id(0)

    @pl.when(step == 0)
    def _():
        acc_ref[...] = jnp.zeros_like(acc_ref)

    acc_ref[...] += wide3(split(tile_of(slab_ref) if lies else slab_ref[...]), split(block_rows(pieces)))

    @pl.when(step == steps - 1)
    def _():
        made = acc_ref[...].T
        proj_ref[...] = made + before[...] if started else made


def project(slab, pieces, at=0, before=None, lies=False):
    nev = slab.shape[0]
    mine, width = pieces[0].shape[1:]
    steps = width // TILE
    rows = 2 * mine * len(pieces)
    out = jax.ShapeDtypeStruct((rows, nev), F32)
    small = [] if before is None else [before]
    return call(
        functools.partial(project_kernel, steps, lies, bool(small)),
        steps,
        [held(slab) if lies else still(slab), *small, *pieces],
        [HELD if lies else columns(slab, at)] + [whole(x) for x in small] + [columns(p) for p in pieces],
        out,
        whole(out),
        "project",
        [pltpu.VMEM((nev, rows), F32)],
    )


def cross_kernel(steps, first, count, slab_ref, *refs):
    *pieces, both_ref, gram_ref, acc_ref = refs
    step = pl.program_id(0)

    @pl.when(step == 0)
    def _():
        gram_ref[...] = jnp.zeros_like(gram_ref)
        acc_ref[...] = jnp.zeros_like(acc_ref)

    high, low = split(block_rows(pieces))
    half = high.shape[0] // 2
    gram_ref[...] += wide3((high[half:], low[half:]), (high[:half], low[:half]))
    mine = half // len(pieces)
    pick = lambda x: jnp.concatenate([x[b * half + first * mine :][: count * mine] for b in (0, 1)], axis=0)
    acc_ref[...] += wide3(split(tile_of(slab_ref)), (pick(high), pick(low)))

    @pl.when(step == steps - 1)
    def _():
        made = acc_ref[...].T
        middle = made.shape[1] // 2
        beside = jnp.concatenate([made[:, :middle], made[:, middle:]], axis=0)
        both_ref[...] = jnp.concatenate([gram_ref[...], beside], axis=1)


def cross(slab, pieces, first, count):
    nev, width = slab.shape
    mine = pieces[0].shape[1]
    n, rows = mine * len(pieces), 2 * mine * count
    out = MADE((n, n + nev // 2), F32)
    return call(
        functools.partial(cross_kernel, width // TILE, first, count),
        width // TILE,
        [held(slab), *pieces],
        [HELD] + [columns(p) for p in pieces],
        out,
        whole(out),
        "cross",
        [pltpu.VMEM((n, n), F32), pltpu.VMEM((nev, rows), F32)],
        vmem=24,
    )


def swap_matrix(n, mask):
    row = lax.broadcasted_iota(jnp.int32, (n, n), 0)
    column = lax.broadcasted_iota(jnp.int32, (n, n), 1)
    return jnp.where(column == jnp.bitwise_xor(row, mask), 1.0, 0.0).astype(F32)


def weigh_kernel(mine, col_ref, factors_ref, gram_ref, given_ref, *refs):
    *sums, high_ref, low_ref, rest_ref = refs
    n = factors_ref.shape[1]
    row = lax.broadcasted_iota(jnp.int32, (n, n), 0)
    column = lax.broadcasted_iota(jnp.int32, (n, n), 1)
    swap = swap_matrix(n, col_ref[0] * mine)
    one, two = (exact(swap, exact(jnp.where(row <= column, factors_ref[b], 0.0), swap)) for b in (0, 1))
    turn = swap_matrix(n, 2 * mine)
    middle = jnp.logical_and(col_ref[0] >= 2, col_ref[0] < 6)
    gram = jnp.where(middle, gram_ref[...], exact(turn, exact(given_ref[...], turn)))
    parts = [x[...] for x in sums]
    known = [jnp.concatenate([x[b * x.shape[0] // 2 :][: x.shape[0] // 2] for x in parts], axis=0) for b in (0, 1)]
    kept = known[0].shape[0]
    none = jnp.zeros((n, n - kept), F32)
    first = jnp.concatenate([exact(one[:, :kept], known[0]), one[:, kept:], none], axis=1)
    second = jnp.concatenate([exact(two[:, :kept], known[1]), none, two[:, kept:]], axis=1)
    second = second - exact(two, exact(gram, first))
    high_ref[...], low_ref[...] = split(jnp.concatenate([first[:kept], second[:kept]], axis=0).T)
    rest_ref[...] = jnp.concatenate([first[kept:], second[kept:]], axis=0)


def weigh(col, factors, gram, given, known0, known1, mine):
    n, nev = 2 * gram.shape[0], known0.shape[1]
    kept = known0.shape[0] + known1.shape[0]
    small = [factors, gram, given, known0, known1]
    outs = [jax.ShapeDtypeStruct((nev + n - kept, kept), BF16)] * 2 + [jax.ShapeDtypeStruct((n - kept, nev + n - kept), F32)]
    return call(
        functools.partial(weigh_kernel, mine),
        1,
        [col[None], *small],
        [pl.BlockSpec(memory_space=pltpu.SMEM)] + [whole(x) for x in small],
        outs,
        [whole(x) for x in outs],
        "weigh",
    )


def apply_kernel(nev, steps, count, high_ref, low_ref, slab_ref, *refs):
    *pieces, a_ref, b_ref, part_ref, xh_ref, xl_ref, last_ref, acc_ref = refs
    step = pl.program_id(0)
    high, low = split(block_rows(pieces))
    left = jnp.concatenate([high_ref[...], low_ref[...], high_ref[...]], axis=1)
    made = lax.dot_general(left, jnp.concatenate([high, high, low], axis=0), NN, preferred_element_type=F32)
    part_ref[...] = slab_ref[...] - made[:nev]
    xh_ref[...], xl_ref[...] = split(made[nev:])

    @pl.when(step == 0)
    def _():
        acc_ref[...] = jnp.zeros_like(acc_ref)

    @pl.when(step < count)
    def _():
        acc_ref[...] += wide3(split(slab_ref[...]), split(block_rows([a_ref, b_ref])))

    @pl.when(step == steps - 1)
    def _():
        last_ref[...] = acc_ref[...].T


def apply(high, low, slab, pieces, late):
    nev, width = slab.shape
    rest, count = high.shape[0] - nev, late[0].shape[-1] // TILE
    outs = [pltpu.VMEM(slab.shape, F32)] + [pltpu.VMEM((rest, width), BF16)] * 2
    last = MADE((rest, nev), F32)
    steps = width // TILE
    return call(
        functools.partial(apply_kernel, nev, steps, count),
        steps,
        [high, low, still(slab), *[still(x) for x in pieces], *late],
        [whole(high), whole(low), columns(slab)]
        + [columns(x) for x in pieces]
        + [pl.BlockSpec((*x.shape[:-1], TILE), lambda g: (0, 0, jnp.minimum(g, count - 1))) for x in late],
        outs + [last],
        [columns(x) for x in outs] + [whole(last)],
        "apply",
        [pltpu.VMEM((nev, rest), F32)],
        vmem=22,
    )


def finish_kernel(starts, part_ref, xh_ref, xl_ref, rest_ref, *refs):
    lasts, (*pieces, out_ref, left_ref) = refs[:4], refs[4:]
    step = pl.program_id(0)
    nev = part_ref.shape[0]

    @pl.when(step == 0)
    def _():
        last = total(lasts)
        more = rest_ref[:, :nev] + exact(rest_ref[:, nev:], last)
        high, low = split(jnp.concatenate([last, more], axis=0).T)
        left_ref[...] = jnp.concatenate([high, low, high], axis=1)

    each = len(pieces) // (len(starts) - 1)
    for i in range(len(starts) - 1):

        @pl.when(jnp.logical_and(step >= starts[i], step < starts[i + 1]))
        def _():
            high, low = split(block_rows(pieces[each * i : each * (i + 1)]))
            high, low = jnp.concatenate([tile_of(xh_ref), high], axis=0), jnp.concatenate([tile_of(xl_ref), low], axis=0)
            right = jnp.concatenate([high, high, low], axis=0)
            out_ref[...] = tile_of(part_ref) - lax.dot_general(left_ref[...], right, NN, preferred_element_type=F32)


def finish(part, xh, xl, rest, lasts, parts):
    nev, width = part.shape
    starts, specs = [0], []
    for pieces in parts:
        first, count = starts[-1], pieces[0].shape[-1] // TILE
        starts.append(first + count)
        specs += [
            pl.BlockSpec((*x.shape[:-1], TILE), lambda g, first=first, count=count: (0, 0, jnp.clip(g - first, 0, count - 1)))
            for x in pieces
        ]
    out = jax.ShapeDtypeStruct(part.shape, F32)
    return call(
        functools.partial(finish_kernel, starts),
        width // TILE,
        [held(part), held(xh), held(xl), rest, *lasts, *[x for pieces in parts for x in pieces]],
        [HELD] * 3 + [whole(rest)] + [whole(x) for x in lasts] + specs,
        out,
        columns(out),
        "finish",
        [pltpu.VMEM((nev, 6 * rest.shape[0]), BF16)],
        vmem=FINISH,
    )


def others(x):
    return [lax.ppermute(x, "row", [(i, i ^ k) for i in range(4)]) for k in (1, 2, 3)]


def cores(pairs):
    return [(2 * a + c, 2 * b + c) for a, b in pairs for c in (0, 1)]


PAIR = cores([(0, 1), (1, 0), (2, 3), (3, 2)])
MIDDLE = cores([(1, 2), (2, 1)])
OUTWARD = cores([(1, 0), (2, 3)])
SIBLING = [(i, i ^ 1) for i in range(8)]


def along(x, pairs):
    return lax.ppermute(x, "col", pairs)


def line_of_four(slab, householder, factors):
    col = lax.axis_index("col")
    mine, width = householder.shape[1:]
    swap = lambda x: along(x, SIBLING)
    other = swap(householder)

    beside, inner = along(householder, PAIR), along(householder, MIDDLE)
    across, outer = along(beside, MIDDLE), along(inner, OUTWARD)
    inner2 = swap(inner)

    kept = hold(slab)
    near = [householder, other, beside, swap(beside)]
    p0 = project(kept, near, lies=True)
    known0 = settle(p0, *others(p0))
    stretches = [(sum(WIDTHS[:i]) * TILE, w * TILE) for i, w in enumerate(WIDTHS)]
    third, cut = join(across, outer, WIDTHS[0], known0)
    fourth = [along(cut, PAIR)]
    near += [third, swap(third)]
    both = cross(kept, near + [inner, inner2], 4, 2)
    gram, known1 = settle_both([both, *others(both)], 4 * mine, slab.shape[0])
    given = along(gram, OUTWARD)
    fourth += [along(take(third, *stretch, given), PAIR) for stretch in stretches[1:]]
    high, low, rest = weigh(col, factors, gram, given, known0, known1, mine)

    fourth[0] = take(fourth[0], 0, stretches[0][1], given)
    parts = [[fourth[0], swap(fourth[0])]]
    *parted, last = apply(high, low, slab, near, parts[0])
    for (at, w), x in zip(stretches[1:], fourth[1:]):
        x = take(x, 0, w, last)
        parts.append([x, swap(x)])
        last = project(slab, parts[-1], at, last)
    return finish(*parted, rest, [last, *others(last)], parts)


def any_mesh(slab, householder, factors):
    upper = jnp.triu(factors)
    for block in range(householder.shape[0]):
        vectors = lax.all_gather(householder[block], "col", axis=0, tiled=True)
        projection = lax.psum(exact(vectors, slab, NT), "row")
        coeffs = exact(upper[block], projection)
        slab = slab - exact(coeffs, vectors, (((0,), (0,)), ((), ())))
    return slab


def solution(mesh):
    small = mesh.shape["col"] == 8 and mesh.shape["row"] == 4
    return jax.shard_map(
        line_of_four if small else any_mesh,
        mesh=mesh,
        in_specs=(P("col", "row"), P(None, "col", "row"), P()),
        out_specs=P("col", "row"),
        check_vma=False,
    )
```

```python
import functools

import jax
import jax.numpy as jnp
from jax import lax
from jax.experimental import pallas as pl
from jax.experimental.pallas import tpu as pltpu
from jax.sharding import PartitionSpec as P

F32 = jnp.float32
BF16 = jnp.bfloat16
NT = (((1,), (1,)), ((), ()))
NN = (((1,), (0,)), ((), ()))
MIB = 1024 * 1024
TILE = 2560
FTILE = 5120
WIDTHS = (4, 2)
COST = dict(settle=10**6, hold=10**9, join=10**6, take=10**6, project=10**9, cross=10**9, weigh=10**6, apply=10**9, finish=10**9)
FINISH = 24
MADE = jax.ShapeDtypeStruct


def split(x):
    high = x.astype(BF16)
    return high, (x - high.astype(F32)).astype(BF16)


def wide3(left, right):
    (lh, ll), (rh, rl) = left, right
    dot = functools.partial(lax.dot_general, dimension_numbers=NT, preferred_element_type=F32)
    n = rh.shape[0]
    both = dot(lh, jnp.concatenate([rh, rl], axis=0))
    return both[:, :n] + (both[:, n:] + dot(ll, rh))


def exact(left, right, dims=NN):
    return lax.dot_general(left, right, dims, precision=lax.Precision.HIGHEST, preferred_element_type=F32)


def block_rows(refs):
    return jnp.concatenate([r[b] for b in (0, 1) for r in refs], axis=0)


def total(refs):
    a, b, c, d = (r[...] for r in refs)
    return (a + b) + (c + d)


def whole(x):
    return pl.BlockSpec(x.shape, lambda g: (0,) * x.ndim)


def columns(x, at=0, tile=TILE):
    lead = x.shape[:-1]
    return pl.BlockSpec(lead + (tile,), lambda g: (0,) * len(lead) + (at // tile + g,))


HELD = pl.BlockSpec(memory_space=pltpu.VMEM)


def held(x):
    return pltpu.with_memory_space_constraint(x, pltpu.VMEM)


def tile_of(ref, tile=TILE):
    return ref[:, pl.ds(pl.multiple_of(pl.program_id(0) * tile, tile), tile)]


def call(kernel, steps, operands, specs, outs, out_specs, name, scratch=(), vmem=16):
    return pl.pallas_call(
        kernel,
        out_shape=outs,
        grid=(steps,),
        in_specs=specs,
        out_specs=out_specs,
        scratch_shapes=list(scratch),
        compiler_params=pltpu.CompilerParams(vmem_limit_bytes=vmem * MIB),
        cost_estimate=pl.CostEstimate(flops=COST[name], bytes_accessed=1, transcendentals=0),
        name=name,
    )(*operands)


def still(x):
    return pltpu.with_memory_space_constraint(x, pltpu.HBM)


def corner(x):
    lead = x.ndim - 2
    return pl.BlockSpec((1,) * lead + (8, 128), lambda g: (0,) * x.ndim)


def join_kernel(count, a_ref, b_ref, *refs):
    out_ref, cut_ref = refs[-2:]
    out_ref[...] = a_ref[...] + b_ref[...]

    @pl.when(pl.program_id(0) < count)
    def _():
        cut_ref[...] = out_ref[...]


def join(a, b, count, *after):
    out, cut = MADE(a.shape, F32), MADE((*a.shape[:-1], count * TILE), F32)
    return call(
        functools.partial(join_kernel, count),
        a.shape[-1] // TILE,
        [a, b, *after],
        [columns(a), columns(b)] + [corner(y) for y in after],
        [out, cut],
        [columns(out), pl.BlockSpec((*a.shape[:-1], TILE), lambda g: (0, 0, jnp.minimum(g, count - 1)))],
        "join",
    )


def hold_kernel(x_ref, out_ref):
    out_ref[...] = x_ref[...]


def hold(x):
    out = pltpu.VMEM(x.shape, F32)
    return call(hold_kernel, x.shape[-1] // TILE, [still(x)], [columns(x)], out, columns(x), "hold")


def settle_kernel(*refs):
    refs[-1][...] = total(refs[:-1])


def settle(*parts):
    return call(settle_kernel, 1, parts, [whole(x) for x in parts], MADE(parts[0].shape, F32), whole(parts[0]), "settle")


def settle_both_kernel(a_ref, b_ref, c_ref, d_ref, gram_ref, proj_ref):
    n, rows = gram_ref.shape[0], proj_ref.shape[0]
    both = total([a_ref, b_ref, c_ref, d_ref])
    gram_ref[...] = both[:, :n]
    proj_ref[...] = jnp.concatenate([both[:rows, n:], both[rows:, n:]], axis=1)


def settle_both(parts, rows, nev):
    n = parts[0].shape[0]
    outs = [MADE((n, n), F32), MADE((rows, nev), F32)]
    return call(settle_both_kernel, 1, parts, [whole(x) for x in parts], outs, [whole(x) for x in outs], "settle")


def take_kernel(x_ref, *refs):
    refs[-1][...] = x_ref[...]


def take(x, at, width, *after):
    out = jax.ShapeDtypeStruct((*x.shape[:-1], width), F32)
    return call(
        take_kernel, width // TILE, [x, *after], [columns(x, at)] + [corner(y) for y in after], out, columns(out), "take"
    )


def project_kernel(steps, lies, started, slab_ref, *refs):
    before, refs = (refs[0], refs[1:]) if started else (None, refs)
    *pieces, proj_ref, acc_ref = refs
    step = pl.program_id(0)

    @pl.when(step == 0)
    def _():
        acc_ref[...] = jnp.zeros_like(acc_ref)

    acc_ref[...] += wide3(split(tile_of(slab_ref) if lies else slab_ref[...]), split(block_rows(pieces)))

    @pl.when(step == steps - 1)
    def _():
        made = acc_ref[...].T
        proj_ref[...] = made + before[...] if started else made


def project(slab, pieces, at=0, before=None, lies=False):
    nev = slab.shape[0]
    mine, width = pieces[0].shape[1:]
    steps = width // TILE
    rows = 2 * mine * len(pieces)
    out = jax.ShapeDtypeStruct((rows, nev), F32)
    small = [] if before is None else [before]
    return call(
        functools.partial(project_kernel, steps, lies, bool(small)),
        steps,
        [held(slab) if lies else still(slab), *small, *pieces],
        [HELD if lies else columns(slab, at)] + [whole(x) for x in small] + [columns(p) for p in pieces],
        out,
        whole(out),
        "project",
        [pltpu.VMEM((nev, rows), F32)],
    )


def cross_kernel(steps, first, count, slab_ref, *refs):
    *pieces, both_ref, gram_ref, acc_ref = refs
    step = pl.program_id(0)

    @pl.when(step == 0)
    def _():
        gram_ref[...] = jnp.zeros_like(gram_ref)
        acc_ref[...] = jnp.zeros_like(acc_ref)

    high, low = split(block_rows(pieces))
    half = high.shape[0] // 2
    gram_ref[...] += wide3((high[half:], low[half:]), (high[:half], low[:half]))
    mine = half // len(pieces)
    pick = lambda x: jnp.concatenate([x[b * half + first * mine :][: count * mine] for b in (0, 1)], axis=0)
    acc_ref[...] += wide3(split(tile_of(slab_ref)), (pick(high), pick(low)))

    @pl.when(step == steps - 1)
    def _():
        made = acc_ref[...].T
        middle = made.shape[1] // 2
        beside = jnp.concatenate([made[:, :middle], made[:, middle:]], axis=0)
        both_ref[...] = jnp.concatenate([gram_ref[...], beside], axis=1)


def cross(slab, pieces, first, count):
    nev, width = slab.shape
    mine = pieces[0].shape[1]
    n, rows = mine * len(pieces), 2 * mine * count
    out = MADE((n, n + nev // 2), F32)
    return call(
        functools.partial(cross_kernel, width // TILE, first, count),
        width // TILE,
        [held(slab), *pieces],
        [HELD] + [columns(p) for p in pieces],
        out,
        whole(out),
        "cross",
        [pltpu.VMEM((n, n), F32), pltpu.VMEM((nev, rows), F32)],
        vmem=24,
    )


def swap_matrix(n, mask):
    row = lax.broadcasted_iota(jnp.int32, (n, n), 0)
    column = lax.broadcasted_iota(jnp.int32, (n, n), 1)
    return jnp.where(column == jnp.bitwise_xor(row, mask), 1.0, 0.0).astype(F32)


def weigh_kernel(mine, col_ref, factors_ref, gram_ref, given_ref, *refs):
    *sums, high_ref, low_ref, rest_ref = refs
    n = factors_ref.shape[1]
    row = lax.broadcasted_iota(jnp.int32, (n, n), 0)
    column = lax.broadcasted_iota(jnp.int32, (n, n), 1)
    swap = swap_matrix(n, col_ref[0] * mine)
    one, two = (exact(swap, exact(jnp.where(row <= column, factors_ref[b], 0.0), swap)) for b in (0, 1))
    turn = swap_matrix(n, 2 * mine)
    middle = jnp.logical_and(col_ref[0] >= 2, col_ref[0] < 6)
    gram = jnp.where(middle, gram_ref[...], exact(turn, exact(given_ref[...], turn)))
    parts = [x[...] for x in sums]
    known = [jnp.concatenate([x[b * x.shape[0] // 2 :][: x.shape[0] // 2] for x in parts], axis=0) for b in (0, 1)]
    kept = known[0].shape[0]
    none = jnp.zeros((n, n - kept), F32)
    first = jnp.concatenate([exact(one[:, :kept], known[0]), one[:, kept:], none], axis=1)
    second = jnp.concatenate([exact(two[:, :kept], known[1]), none, two[:, kept:]], axis=1)
    second = second - exact(two, exact(gram, first))
    high_ref[...], low_ref[...] = split(jnp.concatenate([first[:kept], second[:kept]], axis=0).T)
    rest_ref[...] = jnp.concatenate([first[kept:], second[kept:]], axis=0)


def weigh(col, factors, gram, given, known0, known1, mine):
    n, nev = 2 * gram.shape[0], known0.shape[1]
    kept = known0.shape[0] + known1.shape[0]
    small = [factors, gram, given, known0, known1]
    outs = [jax.ShapeDtypeStruct((nev + n - kept, kept), BF16)] * 2 + [jax.ShapeDtypeStruct((n - kept, nev + n - kept), F32)]
    return call(
        functools.partial(weigh_kernel, mine),
        1,
        [col[None], *small],
        [pl.BlockSpec(memory_space=pltpu.SMEM)] + [whole(x) for x in small],
        outs,
        [whole(x) for x in outs],
        "weigh",
    )


def apply_kernel(nev, steps, count, high_ref, low_ref, slab_ref, *refs):
    *pieces, a_ref, b_ref, part_ref, xh_ref, xl_ref, last_ref, acc_ref = refs
    step = pl.program_id(0)
    high, low = split(block_rows(pieces))
    left = jnp.concatenate([high_ref[...], low_ref[...], high_ref[...]], axis=1)
    made = lax.dot_general(left, jnp.concatenate([high, high, low], axis=0), NN, preferred_element_type=F32)
    part_ref[...] = slab_ref[...] - made[:nev]
    xh_ref[...], xl_ref[...] = split(made[nev:])

    @pl.when(step == 0)
    def _():
        acc_ref[...] = jnp.zeros_like(acc_ref)

    @pl.when(step < count)
    def _():
        acc_ref[...] += wide3(split(slab_ref[...]), split(block_rows([a_ref, b_ref])))

    @pl.when(step == steps - 1)
    def _():
        last_ref[...] = acc_ref[...].T


def apply(high, low, slab, pieces, late):
    nev, width = slab.shape
    rest, count = high.shape[0] - nev, late[0].shape[-1] // TILE
    outs = [pltpu.VMEM(slab.shape, F32)] + [pltpu.VMEM((rest, width), BF16)] * 2
    last = MADE((rest, nev), F32)
    steps = width // TILE
    return call(
        functools.partial(apply_kernel, nev, steps, count),
        steps,
        [high, low, still(slab), *[still(x) for x in pieces], *late],
        [whole(high), whole(low), columns(slab)]
        + [columns(x) for x in pieces]
        + [pl.BlockSpec((*x.shape[:-1], TILE), lambda g: (0, 0, jnp.minimum(g, count - 1))) for x in late],
        outs + [last],
        [columns(x) for x in outs] + [whole(last)],
        "apply",
        [pltpu.VMEM((nev, rest), F32)],
        vmem=22,
    )


def finish_kernel(starts, part_ref, xh_ref, xl_ref, rest_ref, *refs):
    lasts, (*pieces, out_ref, left_ref) = refs[:4], refs[4:]
    step = pl.program_id(0)
    nev = part_ref.shape[0]

    @pl.when(step == 0)
    def _():
        last = total(lasts)
        more = rest_ref[:, :nev] + exact(rest_ref[:, nev:], last)
        high, low = split(jnp.concatenate([last, more], axis=0).T)
        left_ref[...] = jnp.concatenate([high, low, high], axis=1)

    each = len(pieces) // (len(starts) - 1)
    for i in range(len(starts) - 1):

        @pl.when(jnp.logical_and(step >= starts[i], step < starts[i + 1]))
        def _():
            high, low = split(block_rows(pieces[each * i : each * (i + 1)]))
            high, low = jnp.concatenate([tile_of(xh_ref, FTILE), high], axis=0), jnp.concatenate([tile_of(xl_ref, FTILE), low], axis=0)
            right = jnp.concatenate([high, high, low], axis=0)
            out_ref[...] = tile_of(part_ref, FTILE) - lax.dot_general(left_ref[...], right, NN, preferred_element_type=F32)


def finish(part, xh, xl, rest, lasts, parts):
    nev, width = part.shape
    starts, specs = [0], []
    for pieces in parts:
        first, count = starts[-1], pieces[0].shape[-1] // FTILE
        starts.append(first + count)
        specs += [
            pl.BlockSpec((*x.shape[:-1], FTILE), lambda g, first=first, count=count: (0, 0, jnp.clip(g - first, 0, count - 1)))
            for x in pieces
        ]
    out = jax.ShapeDtypeStruct(part.shape, F32)
    return call(
        functools.partial(finish_kernel, starts),
        width // FTILE,
        [held(part), held(xh), held(xl), rest, *lasts, *[x for pieces in parts for x in pieces]],
        [HELD] * 3 + [whole(rest)] + [whole(x) for x in lasts] + specs,
        out,
        columns(out, 0, FTILE),
        "finish",
        [pltpu.VMEM((nev, 6 * rest.shape[0]), BF16)],
        vmem=FINISH,
    )


def others(x):
    return [lax.ppermute(x, "row", [(i, i ^ k) for i in range(4)]) for k in (1, 2, 3)]


def cores(pairs):
    return [(2 * a + c, 2 * b + c) for a, b in pairs for c in (0, 1)]


PAIR = cores([(0, 1), (1, 0), (2, 3), (3, 2)])
MIDDLE = cores([(1, 2), (2, 1)])
OUTWARD = cores([(1, 0), (2, 3)])
SIBLING = [(i, i ^ 1) for i in range(8)]


def along(x, pairs):
    return lax.ppermute(x, "col", pairs)


def line_of_four(slab, householder, factors):
    col = lax.axis_index("col")
    mine, width = householder.shape[1:]
    swap = lambda x: along(x, SIBLING)
    other = swap(householder)

    beside, inner = along(householder, PAIR), along(householder, MIDDLE)
    across, outer = along(beside, MIDDLE), along(inner, OUTWARD)
    inner2 = swap(inner)

    kept = hold(slab)
    near = [householder, other, beside, swap(beside)]
    p0 = project(kept, near, lies=True)
    known0 = settle(p0, *others(p0))
    stretches = [(sum(WIDTHS[:i]) * TILE, w * TILE) for i, w in enumerate(WIDTHS)]
    across = take(across, 0, width, known0)
    third, cut = join(across, outer, WIDTHS[0])
    fourth = [along(cut, PAIR)]
    near += [third, swap(third)]
    both = cross(kept, near + [inner, inner2], 4, 2)
    gram, known1 = settle_both([both, *others(both)], 4 * mine, slab.shape[0])
    given = along(gram, OUTWARD)
    fourth += [along(take(third, *stretch, given), PAIR) for stretch in stretches[1:]]
    high, low, rest = weigh(col, factors, gram, given, known0, known1, mine)

    fourth[0] = take(fourth[0], 0, stretches[0][1], given)
    parts = [[fourth[0], swap(fourth[0])]]
    *parted, last = apply(high, low, slab, near, parts[0])
    for (at, w), x in zip(stretches[1:], fourth[1:]):
        x = take(x, 0, w, last)
        parts.append([x, swap(x)])
        last = project(slab, parts[-1], at, last)
    return finish(*parted, rest, [last, *others(last)], parts)


def any_mesh(slab, householder, factors):
    upper = jnp.triu(factors)
    for block in range(householder.shape[0]):
        vectors = lax.all_gather(householder[block], "col", axis=0, tiled=True)
        projection = lax.psum(exact(vectors, slab, NT), "row")
        coeffs = exact(upper[block], projection)
        slab = slab - exact(coeffs, vectors, (((0,), (0,)), ((), ())))
    return slab


def solution(mesh):
    small = mesh.shape["col"] == 8 and mesh.shape["row"] == 4
    return jax.shard_map(
        line_of_four if small else any_mesh,
        mesh=mesh,
        in_specs=(P("col", "row"), P(None, "col", "row"), P()),
        out_specs=P("col", "row"),
        check_vma=False,
    )
```

```python
import functools

import jax
import jax.numpy as jnp
from jax import lax
from jax.experimental import pallas as pl
from jax.experimental.pallas import tpu as pltpu
from jax.sharding import PartitionSpec as P

F32 = jnp.float32
BF16 = jnp.bfloat16
NT = (((1,), (1,)), ((), ()))
NN = (((1,), (0,)), ((), ()))
MIB = 1024 * 1024
TILE = 2560
FTILE = 5120
CTILE = 1280
WIDTHS = (4, 2)
COST = dict(settle=10**6, hold=10**9, join=10**6, take=10**6, project=10**9, cross=10**9, weigh=10**6, apply=10**9, finish=10**9)
FINISH = 24
MADE = jax.ShapeDtypeStruct


def split(x):
    high = x.astype(BF16)
    return high, (x - high.astype(F32)).astype(BF16)


def wide3(left, right):
    (lh, ll), (rh, rl) = left, right
    dot = functools.partial(lax.dot_general, dimension_numbers=NT, preferred_element_type=F32)
    n = rh.shape[0]
    both = dot(lh, jnp.concatenate([rh, rl], axis=0))
    return both[:, :n] + (both[:, n:] + dot(ll, rh))


def exact(left, right, dims=NN):
    return lax.dot_general(left, right, dims, precision=lax.Precision.HIGHEST, preferred_element_type=F32)


def block_rows(refs):
    return jnp.concatenate([r[b] for b in (0, 1) for r in refs], axis=0)


def total(refs):
    a, b, c, d = (r[...] for r in refs)
    return (a + b) + (c + d)


def whole(x):
    return pl.BlockSpec(x.shape, lambda g: (0,) * x.ndim)


def columns(x, at=0, tile=TILE):
    lead = x.shape[:-1]
    return pl.BlockSpec(lead + (tile,), lambda g: (0,) * len(lead) + (at // tile + g,))


HELD = pl.BlockSpec(memory_space=pltpu.VMEM)


def held(x):
    return pltpu.with_memory_space_constraint(x, pltpu.VMEM)


def tile_of(ref, tile=TILE):
    return ref[:, pl.ds(pl.multiple_of(pl.program_id(0) * tile, tile), tile)]


def call(kernel, steps, operands, specs, outs, out_specs, name, scratch=(), vmem=16):
    return pl.pallas_call(
        kernel,
        out_shape=outs,
        grid=(steps,),
        in_specs=specs,
        out_specs=out_specs,
        scratch_shapes=list(scratch),
        compiler_params=pltpu.CompilerParams(vmem_limit_bytes=vmem * MIB),
        cost_estimate=pl.CostEstimate(flops=COST[name], bytes_accessed=1, transcendentals=0),
        name=name,
    )(*operands)


def still(x):
    return pltpu.with_memory_space_constraint(x, pltpu.HBM)


def corner(x):
    lead = x.ndim - 2
    return pl.BlockSpec((1,) * lead + (8, 128), lambda g: (0,) * x.ndim)


def join_kernel(count, a_ref, b_ref, *refs):
    out_ref, cut_ref = refs[-2:]
    out_ref[...] = a_ref[...] + b_ref[...]

    @pl.when(pl.program_id(0) < count)
    def _():
        cut_ref[...] = out_ref[...]


def join(a, b, count, *after):
    out, cut = MADE(a.shape, F32), MADE((*a.shape[:-1], count * TILE), F32)
    return call(
        functools.partial(join_kernel, count),
        a.shape[-1] // TILE,
        [a, b, *after],
        [columns(a), columns(b)] + [corner(y) for y in after],
        [out, cut],
        [columns(out), pl.BlockSpec((*a.shape[:-1], TILE), lambda g: (0, 0, jnp.minimum(g, count - 1)))],
        "join",
    )


def hold_kernel(x_ref, out_ref):
    out_ref[...] = x_ref[...]


def hold(x):
    out = pltpu.VMEM(x.shape, F32)
    return call(hold_kernel, x.shape[-1] // TILE, [still(x)], [columns(x)], out, columns(x), "hold")


def settle_kernel(*refs):
    refs[-1][...] = total(refs[:-1])


def settle(*parts):
    return call(settle_kernel, 1, parts, [whole(x) for x in parts], MADE(parts[0].shape, F32), whole(parts[0]), "settle")


def settle_both_kernel(a_ref, b_ref, c_ref, d_ref, gram_ref, proj_ref):
    n, rows = gram_ref.shape[0], proj_ref.shape[0]
    both = total([a_ref, b_ref, c_ref, d_ref])
    gram_ref[...] = both[:, :n]
    proj_ref[...] = jnp.concatenate([both[:rows, n:], both[rows:, n:]], axis=1)


def settle_both(parts, rows, nev):
    n = parts[0].shape[0]
    outs = [MADE((n, n), F32), MADE((rows, nev), F32)]
    return call(settle_both_kernel, 1, parts, [whole(x) for x in parts], outs, [whole(x) for x in outs], "settle")


def take_kernel(x_ref, *refs):
    refs[-1][...] = x_ref[...]


def take(x, at, width, *after):
    out = jax.ShapeDtypeStruct((*x.shape[:-1], width), F32)
    tile = width if at % width == 0 else TILE
    return call(
        take_kernel,
        width // tile,
        [x, *after],
        [columns(x, at, tile)] + [corner(y) for y in after],
        out,
        columns(out, 0, tile),
        "take",
    )


def project_kernel(steps, lies, started, slab_ref, *refs):
    before, refs = (refs[0], refs[1:]) if started else (None, refs)
    *pieces, proj_ref, acc_ref = refs
    step = pl.program_id(0)

    @pl.when(step == 0)
    def _():
        acc_ref[...] = jnp.zeros_like(acc_ref)

    acc_ref[...] += wide3(split(tile_of(slab_ref) if lies else slab_ref[...]), split(block_rows(pieces)))

    @pl.when(step == steps - 1)
    def _():
        made = acc_ref[...].T
        proj_ref[...] = made + before[...] if started else made


def project(slab, pieces, at=0, before=None, lies=False):
    nev = slab.shape[0]
    mine, width = pieces[0].shape[1:]
    steps = width // TILE
    rows = 2 * mine * len(pieces)
    out = jax.ShapeDtypeStruct((rows, nev), F32)
    small = [] if before is None else [before]
    return call(
        functools.partial(project_kernel, steps, lies, bool(small)),
        steps,
        [held(slab) if lies else still(slab), *small, *pieces],
        [HELD if lies else columns(slab, at)] + [whole(x) for x in small] + [columns(p) for p in pieces],
        out,
        whole(out),
        "project",
        [pltpu.VMEM((nev, rows), F32)],
    )


def cross_kernel(steps, first, count, slab_ref, *refs):
    *pieces, both_ref, gram_ref, acc_ref = refs
    step = pl.program_id(0)

    @pl.when(step == 0)
    def _():
        gram_ref[...] = jnp.zeros_like(gram_ref)
        acc_ref[...] = jnp.zeros_like(acc_ref)

    high, low = split(block_rows(pieces))
    half = high.shape[0] // 2
    gram_ref[...] += wide3((high[half:], low[half:]), (high[:half], low[:half]))
    mine = half // len(pieces)
    pick = lambda x: jnp.concatenate([x[b * half + first * mine :][: count * mine] for b in (0, 1)], axis=0)
    acc_ref[...] += wide3(split(tile_of(slab_ref, CTILE)), (pick(high), pick(low)))

    @pl.when(step == steps - 1)
    def _():
        made = acc_ref[...].T
        middle = made.shape[1] // 2
        beside = jnp.concatenate([made[:, :middle], made[:, middle:]], axis=0)
        both_ref[...] = jnp.concatenate([gram_ref[...], beside], axis=1)


def cross(slab, pieces, first, count):
    nev, width = slab.shape
    mine = pieces[0].shape[1]
    n, rows = mine * len(pieces), 2 * mine * count
    out = MADE((n, n + nev // 2), F32)
    return call(
        functools.partial(cross_kernel, width // CTILE, first, count),
        width // CTILE,
        [held(slab), *pieces],
        [HELD] + [columns(p, 0, CTILE) for p in pieces],
        out,
        whole(out),
        "cross",
        [pltpu.VMEM((n, n), F32), pltpu.VMEM((nev, rows), F32)],
        vmem=16,
    )


def swap_matrix(n, mask):
    row = lax.broadcasted_iota(jnp.int32, (n, n), 0)
    column = lax.broadcasted_iota(jnp.int32, (n, n), 1)
    return jnp.where(column == jnp.bitwise_xor(row, mask), 1.0, 0.0).astype(F32)


def weigh_kernel(mine, col_ref, factors_ref, gram_ref, given_ref, *refs):
    *sums, high_ref, low_ref, rest_ref = refs
    n = factors_ref.shape[1]
    row = lax.broadcasted_iota(jnp.int32, (n, n), 0)
    column = lax.broadcasted_iota(jnp.int32, (n, n), 1)
    swap = swap_matrix(n, col_ref[0] * mine)
    one, two = (exact(swap, exact(jnp.where(row <= column, factors_ref[b], 0.0), swap)) for b in (0, 1))
    turn = swap_matrix(n, 2 * mine)
    middle = jnp.logical_and(col_ref[0] >= 2, col_ref[0] < 6)
    gram = jnp.where(middle, gram_ref[...], exact(turn, exact(given_ref[...], turn)))
    parts = [x[...] for x in sums]
    known = [jnp.concatenate([x[b * x.shape[0] // 2 :][: x.shape[0] // 2] for x in parts], axis=0) for b in (0, 1)]
    kept = known[0].shape[0]
    none = jnp.zeros((n, n - kept), F32)
    first = jnp.concatenate([exact(one[:, :kept], known[0]), one[:, kept:], none], axis=1)
    second = jnp.concatenate([exact(two[:, :kept], known[1]), none, two[:, kept:]], axis=1)
    second = second - exact(two, exact(gram, first))
    high_ref[...], low_ref[...] = split(jnp.concatenate([first[:kept], second[:kept]], axis=0).T)
    rest_ref[...] = jnp.concatenate([first[kept:], second[kept:]], axis=0)


def weigh(col, factors, gram, given, known0, known1, mine):
    n, nev = 2 * gram.shape[0], known0.shape[1]
    kept = known0.shape[0] + known1.shape[0]
    small = [factors, gram, given, known0, known1]
    outs = [jax.ShapeDtypeStruct((nev + n - kept, kept), BF16)] * 2 + [jax.ShapeDtypeStruct((n - kept, nev + n - kept), F32)]
    return call(
        functools.partial(weigh_kernel, mine),
        1,
        [col[None], *small],
        [pl.BlockSpec(memory_space=pltpu.SMEM)] + [whole(x) for x in small],
        outs,
        [whole(x) for x in outs],
        "weigh",
    )


def apply_kernel(nev, steps, count, high_ref, low_ref, slab_ref, *refs):
    *pieces, a_ref, b_ref, part_ref, xh_ref, xl_ref, last_ref, acc_ref = refs
    step = pl.program_id(0)
    high, low = split(block_rows(pieces))
    left = jnp.concatenate([high_ref[...], low_ref[...], high_ref[...]], axis=1)
    made = lax.dot_general(left, jnp.concatenate([high, high, low], axis=0), NN, preferred_element_type=F32)
    part_ref[...] = slab_ref[...] - made[:nev]
    xh_ref[...], xl_ref[...] = split(made[nev:])

    @pl.when(step == 0)
    def _():
        acc_ref[...] = jnp.zeros_like(acc_ref)

    @pl.when(step < count)
    def _():
        acc_ref[...] += wide3(split(slab_ref[...]), split(block_rows([a_ref, b_ref])))

    @pl.when(step == steps - 1)
    def _():
        last_ref[...] = acc_ref[...].T


def apply(high, low, slab, pieces, late):
    nev, width = slab.shape
    rest, count = high.shape[0] - nev, late[0].shape[-1] // TILE
    outs = [pltpu.VMEM(slab.shape, F32)] + [pltpu.VMEM((rest, width), BF16)] * 2
    last = MADE((rest, nev), F32)
    steps = width // TILE
    return call(
        functools.partial(apply_kernel, nev, steps, count),
        steps,
        [high, low, still(slab), *[still(x) for x in pieces], *late],
        [whole(high), whole(low), columns(slab)]
        + [columns(x) for x in pieces]
        + [pl.BlockSpec((*x.shape[:-1], TILE), lambda g: (0, 0, jnp.minimum(g, count - 1))) for x in late],
        outs + [last],
        [columns(x) for x in outs] + [whole(last)],
        "apply",
        [pltpu.VMEM((nev, rest), F32)],
        vmem=22,
    )


def finish_kernel(starts, part_ref, xh_ref, xl_ref, rest_ref, *refs):
    lasts, (*pieces, out_ref, left_ref) = refs[:4], refs[4:]
    step = pl.program_id(0)
    nev = part_ref.shape[0]

    @pl.when(step == 0)
    def _():
        last = total(lasts)
        more = rest_ref[:, :nev] + exact(rest_ref[:, nev:], last)
        high, low = split(jnp.concatenate([last, more], axis=0).T)
        left_ref[...] = jnp.concatenate([high, low, high], axis=1)

    each = len(pieces) // (len(starts) - 1)
    for i in range(len(starts) - 1):

        @pl.when(jnp.logical_and(step >= starts[i], step < starts[i + 1]))
        def _():
            high, low = split(block_rows(pieces[each * i : each * (i + 1)]))
            high, low = jnp.concatenate([tile_of(xh_ref, FTILE), high], axis=0), jnp.concatenate([tile_of(xl_ref, FTILE), low], axis=0)
            right = jnp.concatenate([high, high, low], axis=0)
            out_ref[...] = tile_of(part_ref, FTILE) - lax.dot_general(left_ref[...], right, NN, preferred_element_type=F32)


def finish(part, xh, xl, rest, lasts, parts):
    nev, width = part.shape
    starts, specs = [0], []
    for pieces in parts:
        first, count = starts[-1], pieces[0].shape[-1] // FTILE
        starts.append(first + count)
        specs += [
            pl.BlockSpec((*x.shape[:-1], FTILE), lambda g, first=first, count=count: (0, 0, jnp.clip(g - first, 0, count - 1)))
            for x in pieces
        ]
    out = jax.ShapeDtypeStruct(part.shape, F32)
    return call(
        functools.partial(finish_kernel, starts),
        width // FTILE,
        [held(part), held(xh), held(xl), rest, *lasts, *[x for pieces in parts for x in pieces]],
        [HELD] * 3 + [whole(rest)] + [whole(x) for x in lasts] + specs,
        out,
        columns(out, 0, FTILE),
        "finish",
        [pltpu.VMEM((nev, 6 * rest.shape[0]), BF16)],
        vmem=FINISH,
    )


def others(x):
    return [lax.ppermute(x, "row", [(i, i ^ k) for i in range(4)]) for k in (1, 2, 3)]


def cores(pairs):
    return [(2 * a + c, 2 * b + c) for a, b in pairs for c in (0, 1)]


PAIR = cores([(0, 1), (1, 0), (2, 3), (3, 2)])
MIDDLE = cores([(1, 2), (2, 1)])
OUTWARD = cores([(1, 0), (2, 3)])
SIBLING = [(i, i ^ 1) for i in range(8)]


def along(x, pairs):
    return lax.ppermute(x, "col", pairs)


def line_of_four(slab, householder, factors):
    col = lax.axis_index("col")
    mine, width = householder.shape[1:]
    swap = lambda x: along(x, SIBLING)
    other = swap(householder)

    beside, inner = along(householder, PAIR), along(householder, MIDDLE)
    across, outer = along(beside, MIDDLE), along(inner, OUTWARD)
    inner2 = swap(inner)

    kept = hold(slab)
    near = [householder, other, beside, swap(beside)]
    p0 = project(kept, near, lies=True)
    known0 = settle(p0, *others(p0))
    stretches = [(sum(WIDTHS[:i]) * TILE, w * TILE) for i, w in enumerate(WIDTHS)]
    across = take(across, 0, width, known0)
    third, cut = join(across, outer, WIDTHS[0])
    fourth = [along(cut, PAIR)]
    near += [third, swap(third)]
    both = cross(kept, near + [inner, inner2], 4, 2)
    gram, known1 = settle_both([both, *others(both)], 4 * mine, slab.shape[0])
    given = along(gram, OUTWARD)
    fourth += [along(take(third, *stretch, given), PAIR) for stretch in stretches[1:]]
    high, low, rest = weigh(col, factors, gram, given, known0, known1, mine)

    fourth[0] = take(fourth[0], 0, stretches[0][1], given)
    parts = [[fourth[0], swap(fourth[0])]]
    *parted, last = apply(high, low, slab, near, parts[0])
    for (at, w), x in zip(stretches[1:], fourth[1:]):
        x = take(x, 0, w, last)
        parts.append([x, swap(x)])
        last = project(slab, parts[-1], at, last)
    return finish(*parted, rest, [last, *others(last)], parts)


def any_mesh(slab, householder, factors):
    upper = jnp.triu(factors)
    for block in range(householder.shape[0]):
        vectors = lax.all_gather(householder[block], "col", axis=0, tiled=True)
        projection = lax.psum(exact(vectors, slab, NT), "row")
        coeffs = exact(upper[block], projection)
        slab = slab - exact(coeffs, vectors, (((0,), (0,)), ((), ())))
    return slab


def solution(mesh):
    small = mesh.shape["col"] == 8 and mesh.shape["row"] == 4
    return jax.shard_map(
        line_of_four if small else any_mesh,
        mesh=mesh,
        in_specs=(P("col", "row"), P(None, "col", "row"), P()),
        out_specs=P("col", "row"),
        check_vma=False,
    )
```
